256 devices in a mesh: row: 64 (over z, y, core), col: 4 (over x).
Axes of the slice: x: 4, y: 4, z: 8, core: 2. Of those that a mesh axis runs over, the one named last changes fastest.
Arguments:
- features: bfloat16 [65536, 128], P(('row', 'col')), may hold values from -6 to 6
- weight: bfloat16 [128, 256], replicated, may hold values from -0.5 to 0.5
- tiles: bfloat16 [64, 4, 384, 128, 128], P('row', 'col'), may hold values from -0.0625 to 0.0625
- tile_rows: int32 [64, 4, 384], P('row', 'col'), may hold values from 0 to 7
- tile_cols: int32 [64, 4, 384], P('row', 'col'), may hold values from 0 to 511, as said below
- tile_count: int32 [64, 4], P('row', 'col'), may hold values from 48 to 384, as said below
- block_perm: int32 [512], replicated, may hold values from 0 to 511, as said below
- cotangent: bfloat16 [65536, 256], P(('row', 'col')), may hold values from -6 to 6
Outputs:
- activation: bfloat16 [65536, 256], P(('row', 'col'))
- grad_features: float32 [65536, 128], P(('row', 'col'))
- grad_weight: float32 [128, 256], replicated
The draws below stay inside these ranges and needn't reach their ends.
Inputs may be any that keep to these rules, and one draw needn't show every extreme that they name: `tile_cols`: on device (r, c) every slot's label lies at a block position p with (p // 2) % 4 == c, including unused slots. `tile_count`: some device is full in every draw. `block_perm`: A permutation of the node-block labels.
All inputs are finite; a program needn't handle non-finite values.
Results may differ from the reference program's by a relative error of at most 0.017.
Values may be sent and summed in bfloat16 or wider, within the bound.
A program may use at most 128 MiB of HBM per device.

```python
import jax
import jax.numpy as jnp
from jax import lax

BS = 128
F = 128
H = 256
BLK_DEV = 2
TCAP = 384
NBLK = 512
NODES = 65536
ROWBLK = 8
N_ROW = 64
N_COL = 4


def shared_labels(key):
    return jax.random.permutation(key, NBLK).astype(jnp.int32)


def draw_block_perm(key, part):
    return shared_labels(key)


def draw_tile_cols(key, part):
    labels = shared_labels(key)
    key = jax.random.fold_in(key, 7)
    key_row, key_blk = jax.random.split(key)
    group = jax.random.randint(key_row, (N_ROW, N_COL, TCAP), 0, N_ROW)
    within = jax.random.randint(key_blk, (N_ROW, N_COL, TCAP), 0, BLK_DEV)
    column = jnp.arange(N_COL, dtype=jnp.int32)[None, :, None]
    place = (group * N_COL + column) * BLK_DEV + within
    return labels[place]


def draw_tile_count(key, part):
    key = jax.random.fold_in(key, 11)
    key_load, key_full = jax.random.split(key)
    level = jax.random.randint(key_load, (N_ROW * N_COL,), 0, 256)
    lowest = TCAP // 8
    counts = lowest + (TCAP - lowest) * level * level // 65025
    fullest = jax.random.randint(key_full, (), 0, N_ROW * N_COL)
    counts = jnp.where(jnp.arange(N_ROW * N_COL) == fullest, TCAP, counts)
    return counts.reshape(N_ROW, N_COL).astype(jnp.int32)


def place_ends(values, rng, smallest, high):
    shape = values.shape
    spot = [jax.random.randint(jax.random.fold_in(rng, axis), (), 0, shape[axis]) for axis in range(len(shape))]
    values = values.at[tuple(spot)].set(smallest)
    longest = shape.index(max(shape))
    spot[longest] = (spot[longest] + 1) % shape[longest]
    return values.at[tuple(spot)].set(high)


def block_scale(stream_key, shape, cuts, least, top_value):
    def one(dim, parts):
        draws = jax.random.uniform(jax.random.fold_in(jax.random.fold_in(stream_key, 6), dim), (parts,), jnp.float32, least / len(cuts), top_value / len(cuts))
        return jnp.repeat(jnp.exp(draws), shape[dim] // parts).reshape((-1,) + (1,) * (len(shape) - dim - 1))

    factor_of = one(*cuts[0])
    for cut in cuts[1:]:
        factor_of = factor_of * one(*cut)
    return factor_of


def scatter_about(stream_key, dims, scale, most, shards=(), held_as=jnp.bfloat16):
    gain = block_scale(stream_key, dims, shards, -0.22, 0.18) if shards else 1.0
    drawn = jax.random.normal(stream_key, dims, jnp.float32) * scale * gain
    return jnp.minimum(jnp.maximum(drawn, -most), most).astype(held_as)


def setup_inputs(seed: int = 0) -> dict:
    arg_keys = jax.random.split(jax.random.key(seed), 9)
    features = scatter_about(arg_keys[0], (NODES, F), 1.0, 6.0, ((0, 256),))
    weight = scatter_about(arg_keys[1], (F, H), F ** -0.5, 0.5)
    tiles = scatter_about(arg_keys[2], (N_ROW, N_COL, TCAP, BS, BS), (BS * TCAP * N_COL // (3 * ROWBLK)) ** -0.5, 0.0625, ((0, 64), (1, 4)))
    tile_rows = place_ends(jax.random.randint(arg_keys[3], (N_ROW, N_COL, TCAP), 0, ROWBLK), jax.random.fold_in(arg_keys[3], 1), 0, ROWBLK - 1).astype(jnp.int32)
    tile_cols = draw_tile_cols(jax.random.fold_in(arg_keys[8], 71), 0)
    tile_count = draw_tile_count(jax.random.fold_in(arg_keys[8], 71), 0)
    block_perm = draw_block_perm(jax.random.fold_in(arg_keys[8], 71), 0)
    cotangent = scatter_about(arg_keys[7], (NODES, H), 1.0, 6.0, ((0, 256),))
    return dict(features=features, weight=weight, tiles=tiles, tile_rows=tile_rows, tile_cols=tile_cols, tile_count=tile_count, block_perm=block_perm, cotangent=cotangent)


def gelu_tanh(values):
    return jax.nn.gelu(values, approximate=True)

def reference(features, weight, tiles, tile_rows, tile_cols, tile_count, block_perm, cotangent):
    position = jnp.zeros((NBLK,), jnp.int32).at[block_perm].set(jnp.arange(NBLK, dtype=jnp.int32))
    devices = N_ROW * N_COL
    flat_tiles = tiles.reshape(devices, TCAP, BS, BS)
    flat_rows = tile_rows.reshape(devices, TCAP)
    flat_cols = tile_cols.reshape(devices, TCAP)
    flat_count = tile_count.reshape(devices)
    device_ids = jnp.arange(devices, dtype=jnp.int32)
    slots = jnp.arange(TCAP, dtype=jnp.int32)
    feat_blocks = features.reshape(NBLK, BS, F)
    xs = (flat_tiles, flat_rows, flat_cols, flat_count, device_ids)

    def forward_step(total, item):
        tile, rows, cols, count, dev = item
        global_rows = dev // N_COL * ROWBLK + rows
        picked = feat_blocks[position[cols]].astype(jnp.float32)
        prod = jnp.einsum('tij,tjf->tif', tile.astype(jnp.float32), picked)
        prod = prod * (slots < count).astype(jnp.float32)[:, None, None]
        return (total.at[global_rows].add(prod), None)
    agg_sum, _ = lax.scan(forward_step, jnp.zeros((NBLK, BS, F), jnp.float32), xs)
    aggregated = agg_sum.reshape(NODES, F).astype(jnp.bfloat16)
    pre = jnp.dot(aggregated, weight, preferred_element_type=jnp.float32)
    activation, pull = jax.vjp(gelu_tanh, pre)
    grad_pre = pull(cotangent.astype(jnp.float32))[0].astype(jnp.bfloat16)
    grad_weight = jnp.dot(aggregated.T, grad_pre, preferred_element_type=jnp.float32)
    grad_agg = jnp.dot(grad_pre, weight.T, preferred_element_type=jnp.float32).astype(jnp.bfloat16)
    grad_blocks = grad_agg.reshape(NBLK, BS, F)

    def backward_step(total, item):
        tile, rows, cols, count, dev = item
        global_rows = dev // N_COL * ROWBLK + rows
        picked = grad_blocks[global_rows].astype(jnp.float32)
        prod = jnp.einsum('tji,tjf->tif', tile.astype(jnp.float32), picked)
        prod = prod * (slots < count).astype(jnp.float32)[:, None, None]
        return (total.at[position[cols]].add(prod), None)
    grad_sum, _ = lax.scan(backward_step, jnp.zeros((NBLK, BS, F), jnp.float32), xs)
    return (activation.astype(jnp.bfloat16), grad_sum.reshape(NODES, F), grad_weight)
```

```python
import math

import jax
import jax.numpy as jnp
from jax import lax
from jax.experimental import pallas as pl
from jax.experimental.pallas import tpu as pltpu
from jax.sharding import PartitionSpec as P

MESH = pl.DeviceIdType.MESH
BF = jnp.bfloat16
F32 = jnp.float32

NZ, NY, NX = 8, 4, 4
BS, F, H = 128, 128, 256
TCAP, NBLK, ROWBLK = 384, 512, 8
NPLACE = 1024
ROWS = 256
G1, G2A, G2 = 176, 48, 80
R1, R2A, R2 = 96, 16, 32
NSEM = 256
GELU = math.sqrt(2.0 / math.pi)


class Sends:
    def __init__(self, send_sem, recv_sem, device):
        self.send_sem, self.recv_sem, self.device = send_sem, recv_sem, device
        self.count, self.started, self.landing = 0, [], {}

    def describe(self, number, source, target, device):
        return pltpu.make_async_remote_copy(
            src_ref=source, dst_ref=target, send_sem=self.send_sem.at[number],
            recv_sem=self.recv_sem.at[number], device_id=device, device_id_type=MESH)

    def start(self, name, source, target, device):
        copy = self.describe(self.count, source, target, device)
        copy.start()
        self.started.append(copy)
        self.landing[name] = (self.count, target)
        self.count += 1

    def wait(self, name):
        number, target = self.landing.pop(name)
        self.describe(number, target, target, self.device).wait_recv()

    def drain(self):
        for copy in self.started:
            copy.wait_send()


def prepare(rows_ref, cols_ref, count_ref, perm_ref, table):
    def iota(shape, dim):
        return lax.broadcasted_iota(jnp.int32, shape, dim)

    def total(picked, values, axis):
        return jnp.sum(jnp.where(picked, values, 0), axis=axis, keepdims=True)

    square = (TCAP, TCAP)
    sub, lane = iota(square, 0), iota(square, 1)
    cols = total(sub == lane, cols_ref[...], 1)
    rows = total(sub == lane, rows_ref[...], 1)
    spot = total(perm_ref[...] == cols, iota((TCAP, NBLK), 1), 1)
    key = rows * 128 + spot // 8 * 2 + spot % 2
    key = jnp.where(iota((TCAP, 1), 0) < count_ref[0, 0], key, 2048)
    flat = total(sub == lane, key, 0)
    ahead = (flat < key) | ((flat == key) & (lane < sub))
    rank = total(ahead, 1, 1)
    order = total(rank == lane, sub, 0)
    keys = total(rank == lane, key, 0)
    place = iota((TCAP, NPLACE), 1)
    upto = total(key <= place, 1, 0)
    here = total(key == place, 1, 0)
    last = jnp.where(here > 0, upto - 1, TCAP)
    table[...] = jnp.zeros_like(table)
    table[0:1, :] = jnp.clip(last, 0, TCAP)
    table[1:2, 0:TCAP] = jnp.clip(order, 0, TCAP - 1)
    table[2:3, 0:TCAP] = keys


def pick(index, line, number, most):
    return jnp.minimum(jnp.maximum(index[line, number], 0), most)


def merge(index, raw, merged):
    def step(number, carry):
        total, before = carry
        mine = index[2, number]
        keep = jnp.where(mine == before, 1.0, 0.0).astype(F32)
        total = raw[pick(index, 1, number, TCAP - 1)].astype(F32) + total * keep
        merged[number] = total.astype(BF)
        return total, mine

    lax.fori_loop(0, TCAP, step, (jnp.zeros((BS, BS), F32), jnp.int32(-1)))
    merged[TCAP] = jnp.zeros((BS, BS), BF)


def whole(
    features, weight, tiles, rows_ref, cols_ref, count_ref, perm_ref, cotangent,
    activation, grad_features, grad_weight,
    raw, merged, table, index, near, acc, part, part_in, gt, twin, twin_in, summed,
    y_in, z_out, z_in, far_in, half_in, relay, relay_in, q_out, q_in,
    w1, w1_in, w2, w2_in, w3, w4, w5, local_sem, send_sem, recv_sem,
):
    row, x = lax.axis_index("row"), lax.axis_index("col")
    z, y, core = row // (2 * NY), (row // 2) % NY, row % 2

    def device(dz, dy, dc=0, dx=0):
        there = ((z + dz + NZ) % NZ * NY + (y + dy + NY) % NY) * 2 + (core + dc) % 2
        return there, (x + dx) % NX

    mine8 = y * 2 + core

    def octet(step):
        there = (mine8 + step) % 8
        return (z * NY + there // 2) * 2 + there % 2, x

    fetches = []
    for part_no in range(8):
        some = pl.ds(part_no * (TCAP // 8), TCAP // 8)
        fetches.append(pltpu.make_async_copy(tiles.at[0, 0, some], raw.at[some], local_sem.at[part_no]))
        fetches[-1].start()
    barrier = pltpu.get_barrier_semaphore()
    peers = [device(dz, 0) for dz in range(1, NZ)] + [octet(step) for step in range(1, 8)]
    peers += [device(0, 0, 0, dx) for dx in range(1, NX)]
    for peer in peers:
        pl.semaphore_signal(barrier, inc=1, device_id=peer, device_id_type=MESH)

    prepare(rows_ref, cols_ref, count_ref, perm_ref, table)
    to_scalar = pltpu.make_async_copy(table, index, local_sem.at[8])
    to_scalar.start()
    acc[...] = jnp.zeros_like(acc)
    near[0, 0, 0] = features[...]
    to_scalar.wait()
    for fetch in fetches:
        fetch.wait()
    merge(index, raw, merged)
    pl.semaphore_wait(barrier, len(peers))

    sends = Sends(send_sem, recv_sem, device(0, 0, 1))
    sibling = device(0, 0, 1)

    def block(oz, oy, piece):
        return near.at[oz % NZ, oy % NY, 0, pl.ds(piece[0], piece[1]), :]

    g1, g2, g2a, g2b = (0, G1), (G1, G2), (G1, G2A), (G1 + G2A, G2 - G2A)

    def pass_on(name, oz, oy, piece, dz, dy):
        source = features.at[pl.ds(piece[0], piece[1]), :] if (oz, oy) == (0, 0) else block(oz, oy, piece)
        sends.start(name, source, block(oz - dz, oy - dy, piece), device(dz, dy))

    def along_y(oz):
        for dy in (1, -1, 2):
            pass_on(("y", oz, dy), oz, 0, g1, 0, dy)

    def along_y_done(oz):
        for dy in (1, -1, 2):
            sends.wait(("y", oz, dy))

    def along_z(oy):
        for dz in (1, -1, 2, -2):
            pass_on(("q", oy, dz), 0, oy, g2, dz, 0)

    def along_z_more(oy):
        for s, half in ((1, g2a), (-1, g2b)):
            sends.wait(("q", oy, s))
            sends.wait(("q", oy, 2 * s))
            pass_on(("q", oy, 3 * s), -2 * s, oy, g2, s, 0)
            pass_on(("q", oy, 4 * s), -2 * s, oy, half, 2 * s, 0)

    def share(oz):
        sends.start(("s", oz), near.at[oz % NZ, :, 0], near.at[oz % NZ, :, 1], sibling)

    def column(dzi, dyi, other):
        there = (((z + dzi) % NZ) * NY + (y + dyi) % NY) * 2 + (core + other) % 2
        return there * 2

    def forward(first, second, other):
        def step(number, carry):
            dzi = first + (second - first) * (number // NY)
            dyi = number % NY
            where = column(dzi, dyi, other)
            block_in = near[dzi, dyi, other]
            for rb in range(ROWBLK):
                left = merged[pick(index, 0, rb * 128 + where, TCAP)]
                right = merged[pick(index, 0, rb * 128 + where + 1, TCAP)]
                acc[rb] += jnp.dot(jnp.concatenate([left, right], axis=1), block_in, preferred_element_type=F32)
            return carry

        lax.fori_loop(0, NY if first == second else 2 * NY, step, 0)

    for s in (1, -1):
        pass_on(("z", s), 0, 0, g1, s, 0)
        pass_on(("p", s), 0, 0, g2, 0, s)
    for s in (1, -1):
        pass_on(("z", 2 * s), 0, 0, g1, 2 * s, 0)
    pass_on(("p", 2), 0, 0, g2, 0, 2)
    along_y(0)
    for s in (1, -1):
        pass_on(("z", 3 * s), 0, 0, g1, 3 * s, 0)
    pass_on(("z", 4), 0, 0, g1, 4, 0)
    along_z(0)
    for s in (1, -1):
        sends.wait(("z", s))
        along_y(-s)
    for s in (1, -1):
        sends.wait(("p", s))
        along_z(-s)
    for s in (1, -1):
        sends.wait(("z", 2 * s))
        along_y(-2 * s)
    sends.wait(("p", 2))
    along_z(-2)
    for s in (1, -1):
        sends.wait(("z", 3 * s))
        along_y(-3 * s)
    sends.wait(("z", 4))
    along_y(-4)
    along_y_done(0)
    share(0)
    along_z_more(0)
    forward(0, 0, 0)
    along_z_more(-1)
    along_z_more(1)
    along_z_more(-2)
    for oz in (-1, 1):
        along_y_done(oz)
        share(oz)
    sends.wait(("s", 0))
    forward(0, 0, 1)
    forward(1, 7, 0)
    for oz in (-2, 2):
        along_y_done(oz)
        share(oz)
    sends.wait(("s", 1))
    sends.wait(("s", -1))
    forward(1, 7, 1)
    forward(2, 6, 0)
    for oy in (0, -1, 1, -2):
        sends.wait(("q", oy, 3))
        sends.wait(("q", oy, -3))
    for oz in (-3, 3):
        along_y_done(oz)
        share(oz)
    sends.wait(("s", 2))
    sends.wait(("s", -2))
    forward(2, 6, 1)
    forward(3, 5, 0)
    for oy in (0, -1, 1, -2):
        sends.wait(("q", oy, 4))
        sends.wait(("q", oy, -4))
    along_y_done(-4)
    share(4)
    sends.wait(("s", 3))
    sends.wait(("s", -3))
    forward(3, 5, 1)
    forward(4, 4, 0)
    sends.wait(("s", 4))
    forward(4, 4, 1)

    for dx in (2, 1, 3):
        there = (x + dx) % NX
        part[dx] = acc[pl.ds(there * 2, 2)].reshape(ROWS, F).astype(BF)
        sends.start(("part", dx), part.at[dx], part_in.at[dx], device(0, 0, 0, dx))
    total = acc[pl.ds(x * 2, 2)].reshape(ROWS, F)
    for dx in (1, 3, 2):
        sends.wait(("part", dx))
        total += part_in[dx].astype(F32)
    aggregated = total.astype(BF)
    pre = jnp.dot(aggregated, weight[...], preferred_element_type=F32)
    square = pre * pre
    bend = jnp.tanh(GELU * (pre + 0.044715 * (square * pre)))
    slope = 0.5 * (1.0 + bend) + (0.5 * GELU) * pre * (1.0 - bend * bend) * (1.0 + 3.0 * 0.044715 * square)
    grad_pre = (cotangent[...].astype(F32) * slope).astype(BF)
    gt[0] = lax.dot_general(weight[...], grad_pre, (((1,), (1,)), ((), ())), preferred_element_type=F32).astype(BF)
    for dx in (2, 1, 3):
        sends.start(("gt", dx), gt.at[0], gt.at[NX - dx], device(0, 0, 0, dx))
    activation[...] = (0.5 * pre * (1.0 + bend)).astype(BF)
    term = lax.dot_general(aggregated, grad_pre, (((0,), (0,)), ((), ())), preferred_element_type=F32)
    for q in range(NX):
        for j in range(8):
            w1[q, j] = term[q * 32 + j % 4 * 8:q * 32 + j % 4 * 8 + 8, j // 4 * 128:j // 4 * 128 + 128]
    for dx in (2, 1, 3):
        sends.start(("w1", dx), w1.at[(x + dx) % NX], w1_in.at[dx], device(0, 0, 0, dx))
    for dx in (1, 3, 2):
        sends.wait(("gt", dx))

    def backward(first, second, other):
        def step(number, carry):
            dzi = first + (second - first) * (number // NY)
            dyi = number % NY
            where = column(dzi, dyi, other)
            sum_ = jnp.zeros((F, ROWS), F32)
            for dx in range(NX):
                base = (x + dx) % NX * 2 * 128 + where
                corners = [merged[pick(index, 0, base + a, TCAP)] for a in (0, 1, 128, 129)]
                grid = jnp.concatenate([jnp.concatenate(corners[:2], axis=1), jnp.concatenate(corners[2:], axis=1)], axis=0)
                sum_ += jnp.dot(gt[dx], grid, preferred_element_type=F32)
            if other:
                twin[dzi, dyi] = sum_.astype(BF)
            else:
                summed[dzi, dyi] = (sum_ + twin_in[dzi, dyi].astype(F32)).astype(BF)
            return carry

        lax.fori_loop(0, NY if first == second else 2 * NY, step, 0)

    r1, r2, r2a, r2b = pl.ds(0, R1), pl.ds(R1, R2), pl.ds(R1, R2A), pl.ds(R1 + R2A, R2 - R2A)
    dys = (1, 3, 2)

    def for_twin(*group):
        backward(group[0], group[-1], 1)
        for dzi in group:
            sends.start(("t", dzi), twin.at[dzi], twin_in.at[dzi], sibling)

    def for_plane(*group):
        for dzi in group:
            sends.wait(("t", dzi))
        backward(group[0], group[-1], 0)
        for dzi in group:
            for k, dy in enumerate(dys):
                sends.start(("Y", dzi, k), summed.at[dzi, dy, r1], y_in.at[dzi, k], device(0, dy))
        for dzi in group:
            for dy in range(NY):
                if dzi == 4:
                    sends.start(("half", 0, dy), summed.at[4, dy, r2a], half_in.at[0, dy, pl.ds(0, R2A)], device(2, 0))
                    sends.start(("half", 1, dy), summed.at[4, dy, r2b], half_in.at[1, dy, pl.ds(0, R2 - R2A)], device(-2, 0))
                elif dzi in (3, 5):
                    s = 0 if dzi == 3 else 1
                    sends.start(("far", s, dy), summed.at[dzi, dy, r2], far_in.at[s, dy], device(1 - 2 * s, 0))
                elif dzi in (1, 7):
                    s = 0 if dzi == 1 else 1
                    sends.start(("q", s, dy), summed.at[dzi, dy, r2], relay_in.at[s, dy], device(1 - 2 * s, 0))

    def relays():
        for s, dzi in ((0, 2), (1, 6)):
            for dy in (1, 3, 2, 0):
                sends.wait(("half", s, dy))
                sends.wait(("far", s, dy))
                relay[s, dy] = (summed[dzi, dy, r2].astype(F32) + far_in[s, dy].astype(F32)).astype(BF)
                some = pl.ds(0, R2A) if s == 0 else pl.ds(R2A, R2 - R2A)
                extra = half_in[s, dy, pl.ds(0, R2A if s == 0 else R2 - R2A)]
                mine = r2a if s == 0 else r2b
                relay[s, dy, some] = (
                    summed[dzi, dy, mine].astype(F32) + far_in[s, dy, some].astype(F32) + extra.astype(F32)
                ).astype(BF)
                sends.start(("q", 2 + s, dy), relay.at[s, dy], relay_in.at[2 + s, dy], device(2 - 4 * s, 0))

    def y_sum(dzi):
        value = summed[dzi, 0, r1].astype(F32)
        for k in range(3):
            sends.wait(("Y", dzi, k))
            value += y_in[dzi, k].astype(F32)
        return value

    def z_stage(dzi):
        z_out[dzi] = y_sum(dzi).astype(BF)
        sends.start(("Z", dzi), z_out.at[dzi], z_in.at[dzi], device(dzi, 0))

    def q_sum(dy):
        value = summed[0, dy, r2].astype(F32)
        for k in range(4):
            sends.wait(("q", k, dy))
            value += relay_in[k, dy].astype(F32)
        return value

    for_twin(4)
    for_twin(3, 5)
    for_plane(4)
    for_twin(2, 6)
    for_plane(3, 5)
    w2[...] = w1[x]
    for dx in (1, 3, 2):
        sends.wait(("w1", dx))
        w2[...] += w1_in[dx]
    for step in range(1, 8):
        sends.start(("w2", step), w2.at[(mine8 + step) % 8], w2_in.at[step], octet(step))
    for_twin(1, 7)
    for_plane(2, 6)
    z_stage(4)
    relays()
    for_twin(0)
    for_plane(1, 7)
    z_stage(3)
    z_stage(5)
    here = w2[mine8]
    for step in range(1, 8):
        sends.wait(("w2", step))
        here += w2_in[step]
    w3[z] = here
    for dz in range(1, NZ):
        sends.start(("w3", dz), w3.at[z], w3.at[z], device(dz, 0))
    for_plane(0)
    for dzi in (2, 6, 1, 7):
        z_stage(dzi)
    for k, dy in enumerate(dys):
        q_out[k] = q_sum(dy).astype(BF)
        sends.start(("Q", k), q_out.at[k], q_in.at[k], device(0, dy))
    for dz in range(1, NZ):
        number, _ = sends.landing.pop(("w3", dz))
        source = w3.at[(z + NZ - dz) % NZ]
        sends.describe(number, source, source, sibling).wait_recv()
    here = w3[0]
    for k in range(1, NZ):
        here += w3[k]
    w4[mine8] = here
    for step in range(1, 8):
        sends.start(("w4", step), w4.at[mine8], w4.at[mine8], octet(step))
    top = y_sum(0)
    bottom = q_sum(0)
    for step in range(1, 8):
        number, _ = sends.landing.pop(("w4", step))
        source = w4.at[(mine8 + 8 - step) % 8]
        sends.describe(number, source, source, sibling).wait_recv()
    w5[x] = w4[...]
    for dx in (2, 1, 3):
        sends.start(("w5", dx), w4, w5.at[x], device(0, 0, 0, dx))
    for dzi in (4, 3, 5, 2, 6, 1, 7):
        sends.wait(("Z", dzi))
        top += z_in[dzi].astype(F32)
    for k in range(3):
        sends.wait(("Q", k))
        bottom += q_in[k].astype(F32)
    grad_features[...] = jnp.concatenate([top, bottom], axis=0).T
    for dx in (1, 3, 2):
        number, _ = sends.landing.pop(("w5", dx))
        source = w5.at[(x + NX - dx) % NX]
        sends.describe(number, source, source, sibling).wait_recv()
    for q in range(NX):
        for j in range(8):
            grad_weight[pl.ds(q * 32 + j % 4 * 8, 8), pl.ds(j // 4 * 128, 128)] = w5[q, j]
    sends.drain()
    assert not sends.landing


def body(features, weight, tiles, tile_rows, tile_cols, tile_count, block_perm, cotangent):
    vmem = pl.BlockSpec(memory_space=pltpu.VMEM)
    smem = pl.BlockSpec(memory_space=pltpu.SMEM)
    return pl.pallas_call(
        whole,
        out_shape=(
            jax.ShapeDtypeStruct((ROWS, H), BF),
            jax.ShapeDtypeStruct((ROWS, F), F32),
            jax.ShapeDtypeStruct((F, H), F32),
        ),
        in_specs=[vmem, vmem, pl.BlockSpec(memory_space=pl.ANY), vmem, vmem, smem, vmem, vmem],
        out_specs=(vmem, vmem, vmem),
        scratch_shapes=[
            pltpu.VMEM((TCAP, BS, BS), BF),
            pltpu.VMEM((TCAP + 1, BS, BS), BF),
            pltpu.VMEM((8, NPLACE), jnp.int32),
            pltpu.SMEM((8, NPLACE), jnp.int32),
            pltpu.VMEM((NZ, NY, 2, ROWS, F), BF),
            pltpu.VMEM((ROWBLK, BS, F), F32),
            pltpu.VMEM((NX, ROWS, F), BF),
            pltpu.VMEM((NX, ROWS, F), BF),
            pltpu.VMEM((NX, F, ROWS), BF),
            pltpu.VMEM((NZ, NY, F, ROWS), BF),
            pltpu.VMEM((NZ, NY, F, ROWS), BF),
            pltpu.VMEM((NZ, NY, F, ROWS), BF),
            pltpu.VMEM((NZ, 3, R1, ROWS), BF),
            pltpu.VMEM((NZ, R1, ROWS), BF),
            pltpu.VMEM((NZ, R1, ROWS), BF),
            pltpu.VMEM((2, NY, R2, ROWS), BF),
            pltpu.VMEM((2, NY, R2A, ROWS), BF),
            pltpu.VMEM((2, NY, R2, ROWS), BF),
            pltpu.VMEM((4, NY, R2, ROWS), BF),
            pltpu.VMEM((3, R2, ROWS), BF),
            pltpu.VMEM((3, R2, ROWS), BF),
            pltpu.VMEM((NX, 8, 8, 128), F32),
            pltpu.VMEM((NX, 8, 8, 128), F32),
            pltpu.VMEM((8, 8, 128), F32),
            pltpu.VMEM((8, 8, 128), F32),
            pltpu.VMEM((NZ, 8, 128), F32),
            pltpu.VMEM((8, 8, 128), F32),
            pltpu.VMEM((NX, 8, 8, 128), F32),
            pltpu.SemaphoreType.DMA((9,)),
            pltpu.SemaphoreType.DMA((NSEM,)),
            pltpu.SemaphoreType.DMA((NSEM,)),
        ],
        compiler_params=pltpu.CompilerParams(
            collective_id=0, has_side_effects=True, vmem_limit_bytes=56 * 2**20),
    )(
        features, weight, tiles, tile_rows.reshape(1, TCAP), tile_cols.reshape(1, TCAP), tile_count,
        block_perm.reshape(1, NBLK), cotangent,
    )


def solution(mesh):
    return jax.shard_map(
        body,
        mesh=mesh,
        in_specs=(
            P(("row", "col"), None),
            P(),
            P("row", "col", None, None, None),
            P("row", "col", None),
            P("row", "col", None),
            P("row", "col"),
            P(),
            P(("row", "col"), None),
        ),
        out_specs=(P(("row", "col"), None), P(("row", "col"), None), P()),
        check_vma=False,
    )
```

```python
import math

import jax
import jax.numpy as jnp
from jax import lax
from jax.experimental import pallas as pl
from jax.experimental.pallas import tpu as pltpu
from jax.sharding import PartitionSpec as P

MESH = pl.DeviceIdType.MESH
BF = jnp.bfloat16
F32 = jnp.float32

NZ, NY, NX = 8, 4, 4
BS, F, H = 128, 128, 256
TCAP, NBLK, ROWBLK = 384, 512, 8
NPLACE = 1024
ROWS = 256
G1, G1A, G2A, G2 = 176, 80, 48, 80
R1, R1A, R2A, R2 = 80, 32, 16, 48
NSEM = 256
GELU = math.sqrt(2.0 / math.pi)


class Sends:
    def __init__(self, send_sem, recv_sem, device):
        self.send_sem, self.recv_sem, self.device = send_sem, recv_sem, device
        self.count, self.started, self.landing = 0, [], {}

    def describe(self, number, source, target, device):
        return pltpu.make_async_remote_copy(
            src_ref=source, dst_ref=target, send_sem=self.send_sem.at[number],
            recv_sem=self.recv_sem.at[number], device_id=device, device_id_type=MESH)

    def start(self, name, source, target, device):
        copy = self.describe(self.count, source, target, device)
        copy.start()
        self.started.append(copy)
        self.landing[name] = (self.count, target)
        self.count += 1

    def wait(self, name):
        self.wait_for(name, self.landing[name][1])

    def wait_for(self, name, target):
        number, _ = self.landing.pop(name)
        self.describe(number, target, target, self.device).wait_recv()

    def drain(self):
        for copy in self.started:
            copy.wait_send()


def prepare(rows_ref, cols_ref, count_ref, perm_ref, table):
    def iota(shape, dim):
        return lax.broadcasted_iota(jnp.int32, shape, dim)

    def total(picked, values, axis):
        return jnp.sum(jnp.where(picked, values, 0), axis=axis, keepdims=True)

    square = (TCAP, TCAP)
    sub, lane = iota(square, 0), iota(square, 1)
    cols = total(sub == lane, cols_ref[...], 1)
    rows = total(sub == lane, rows_ref[...], 1)
    spot = total(perm_ref[...] == cols, iota((TCAP, NBLK), 1), 1)
    key = rows * 128 + spot // 8 * 2 + spot % 2
    key = jnp.where(iota((TCAP, 1), 0) < count_ref[...], key, 2048)
    flat = total(sub == lane, key, 0)
    ahead = (flat < key) | ((flat == key) & (lane < sub))
    rank = total(ahead, 1, 1)
    order = total(rank == lane, sub, 0)
    keys = total(rank == lane, key, 0)
    place = iota((TCAP, NPLACE), 1)
    upto = total(key <= place, 1, 0)
    here = total(key == place, 1, 0)
    last = jnp.where(here > 0, upto - 1, TCAP)
    table[...] = jnp.zeros_like(table)
    table[0:1, :] = jnp.clip(last, 0, TCAP)
    table[1:2, 0:TCAP] = jnp.clip(order, 0, TCAP - 1)
    table[2:3, 0:TCAP] = keys


def pick(index, line, number, most):
    return jnp.minimum(jnp.maximum(index[line, number], 0), most)


def merge(index, raw, merged):
    def step(number, carry):
        total, before = carry
        mine = index[2, number]
        keep = jnp.where(mine == before, 1.0, 0.0).astype(F32)
        total = raw[pick(index, 1, number, TCAP - 1)].astype(F32) + total * keep
        merged[number] = total.astype(BF)
        return total, mine

    lax.fori_loop(0, TCAP, step, (jnp.zeros((BS, BS), F32), jnp.int32(-1)), unroll=8)
    merged[TCAP] = jnp.zeros((BS, BS), BF)


def whole(
    features, weight_in, tiles, rows_in, cols_in, count_in, perm_in, cotangent_in,
    activation, grad_turned, w5,
    weight, rows_ref, cols_ref, count_ref, perm_ref, cotangent, raw, merged, table, index, near, acc, part, part_in, gt, twin, twin_in, summed,
    y_in, z_out, z_in, z_far, z_half, far_in, half_in, relay, relay_in, q_out, q_in,
    w1, w1_in, w2, w2_in, w3, w4, local_sem, send_sem, recv_sem,
):
    row, x = lax.axis_index("row"), lax.axis_index("col")
    z, y, core = row // (2 * NY), (row // 2) % NY, row % 2

    def device(dz, dy, dc=0, dx=0):
        there = ((z + dz + NZ) % NZ * NY + (y + dy + NY) % NY) * 2 + (core + dc) % 2
        return there, (x + dx) % NX

    mine8 = y * 2 + core

    def octet(step):
        there = (mine8 + step) % 8
        return (z * NY + there // 2) * 2 + there % 2, x

    lists = [(rows_in, rows_ref), (cols_in, cols_ref), (count_in, count_ref), (perm_in, perm_ref)]
    lists = [pltpu.make_async_copy(*pair, local_sem.at[9 + k]) for k, pair in enumerate(lists)]
    for copy in lists:
        copy.start()
    barrier = pltpu.get_barrier_semaphore()
    peers = [device(dz, 0) for dz in range(1, NZ)] + [octet(step) for step in range(1, 8)]
    peers += [device(0, 0, 0, dx) for dx in range(1, NX)]
    for peer in peers:
        pl.semaphore_signal(barrier, inc=1, device_id=peer, device_id_type=MESH)
    fetches = [pltpu.make_async_copy(features, near.at[0, 0, 0], local_sem.at[13])]
    for part_no in range(8):
        some = pl.ds(part_no * (TCAP // 8), TCAP // 8)
        fetches.append(pltpu.make_async_copy(tiles.at[0, 0, some], raw.at[some], local_sem.at[part_no]))
    fetches.append(pltpu.make_async_copy(weight_in, weight, local_sem.at[14]))
    fetches.append(pltpu.make_async_copy(cotangent_in, cotangent, local_sem.at[15]))
    for fetch in fetches:
        fetch.start()
    for copy in lists:
        copy.wait()
    prepare(rows_ref, cols_ref, count_ref, perm_ref, table)
    to_scalar = pltpu.make_async_copy(table, index, local_sem.at[8])
    to_scalar.start()
    acc[...] = jnp.zeros_like(acc)
    pl.semaphore_wait(barrier, len(peers))

    sends = Sends(send_sem, recv_sem, device(0, 0, 1))
    sibling = device(0, 0, 1)

    def block(oz, oy, piece):
        return near.at[oz % NZ, oy % NY, 0, pl.ds(piece[0], piece[1]), :]

    g1, g1a, g1b = (0, G1), (0, G1A), (G1A, G1 - G1A)
    g2, g2a, g2b = (G1, G2), (G1, G2A), (G1 + G2A, G2 - G2A)

    def pass_on(name, oz, oy, piece, dz, dy):
        source = features.at[pl.ds(piece[0], piece[1]), :] if (oz, oy) == (0, 0) else block(oz, oy, piece)
        sends.start(name, source, block(oz - dz, oy - dy, piece), device(dz, dy))

    def along_y(oz, relayed):
        for dy in (1, -1):
            pass_on(("y", oz, dy), oz, 0, g1, 0, dy)
        if not relayed:
            pass_on(("y", oz, 2), oz, 0, g1, 0, 2)

    def along_y_more(oz):
        for s, half in ((1, g1a), (-1, g1b)):
            sends.wait(("y", oz, s))
            pass_on(("y", oz, 2 * s), oz, -s, half, 0, s)

    def along_y_done(oz, relayed):
        for dy in (2, -2) if relayed else (1, -1, 2):
            sends.wait(("y", oz, dy))

    def along_z(name, oy, piece, dzs):
        for dz in dzs:
            pass_on((name, oy, dz), 0, oy, piece, dz, 0)

    def along_z_more(name, oy, piece, halves):
        for s, half in ((1, halves[0]), (-1, halves[1])):
            sends.wait((name, oy, 2 * s))
            pass_on((name, oy, 3 * s), -2 * s, oy, piece, s, 0)
            pass_on((name, oy, 4 * s), -2 * s, oy, half, 2 * s, 0)

    def q_more(oy):
        along_z_more("q", oy, g2, (g2a, g2b))

    def q_done(*dzs):
        for oy in (0, -1, 1, 2):
            for dz in dzs:
                sends.wait(("q", oy, dz))

    def share(oz):
        sends.start(("s", oz), near.at[oz % NZ, :, 0], near.at[oz % NZ, :, 1], sibling)

    def shared(*ozs):
        for oz in ozs:
            sends.wait(("s", oz))

    def column(dzi, dyi, other):
        there = (((z + dzi) % NZ) * NY + (y + dyi) % NY) * 2 + (core + other) % 2
        return there * 2

    def forward(first, second, other):
        def step(number, carry):
            dzi = first + (second - first) * number
            for part_no in range(0, ROWBLK, 4):
                sum_ = jnp.zeros((4 * BS, F), F32)
                for dyi in range(NY):
                    where = column(dzi, dyi, other)
                    left = [merged[pick(index, 0, rb * 128 + where, TCAP)] for rb in range(part_no, part_no + 4)]
                    right = [merged[pick(index, 0, rb * 128 + where + 1, TCAP)] for rb in range(part_no, part_no + 4)]
                    both = jnp.concatenate([jnp.concatenate(left, axis=0), jnp.concatenate(right, axis=0)], axis=1)
                    sum_ += jnp.dot(both, near[dzi, dyi, other], preferred_element_type=F32)
                acc[pl.ds(part_no, 4)] += sum_.reshape(4, BS, F)
            return carry

        lax.fori_loop(0, 1 if first == second else 2, step, 0)

    along_z("z", 0, g1, (2, -2, 1, -1))
    for s in (1, -1):
        pass_on(("p", s), 0, 0, g2, 0, s)
    along_y(0, True)
    pass_on(("p", 2), 0, 0, g2, 0, 2)
    along_z("q", 0, g2, (2, -2, 1, -1))
    to_scalar.wait()
    for fetch in fetches:
        fetch.wait()
    merge(index, raw, merged)
    for s in (1, -1):
        sends.wait(("z", 0, s))
        along_y(-s, True)
    along_z_more("z", 0, g1, (g1a, g1b))
    for s in (1, -1):
        sends.wait(("p", s))
        along_z("q", -s, g2, (2, -2, 1, -1))
    sends.wait(("p", 2))
    along_z("q", 2, g2, (2, -2, 1, -1))
    for s in (1, -1):
        along_y(2 * s, True)
    along_y_more(0)
    q_more(0)
    along_y_more(-1)
    along_y_more(1)
    for s in (1, -1):
        sends.wait(("z", 0, 3 * s))
        along_y(-3 * s, False)
    for s in (1, -1):
        sends.wait(("z", 0, 4 * s))
    along_y(4, False)
    q_more(-1)
    q_more(1)
    along_y_done(0, True)
    share(0)
    along_y_more(-2)
    along_y_more(2)
    q_more(2)
    forward(0, 0, 0)
    q_done(1, -1)
    for oz in (-1, 1):
        along_y_done(oz, True)
        share(oz)
    shared(0)
    forward(0, 0, 1)
    forward(1, 7, 0)
    for oz in (-2, 2):
        along_y_done(oz, True)
        share(oz)
    shared(1, -1)
    forward(1, 7, 1)
    forward(2, 6, 0)
    shared(2, -2)
    forward(2, 6, 1)
    q_done(3, -3)
    for oz in (-3, 3):
        along_y_done(oz, False)
        share(oz)
    forward(3, 5, 0)
    q_done(4, -4)
    along_y_done(4, False)
    share(4)
    shared(3, -3)
    forward(3, 5, 1)
    forward(4, 4, 0)
    shared(4)
    forward(4, 4, 1)

    for dx in (2, 1, 3):
        there = (x + dx) % NX
        part[dx] = acc[pl.ds(there * 2, 2)].reshape(ROWS, F).astype(BF)
        sends.start(("part", dx), part.at[dx], part_in.at[dx], device(0, 0, 0, dx))
    total = acc[pl.ds(x * 2, 2)].reshape(ROWS, F)
    for dx in (1, 3, 2):
        sends.wait(("part", dx))
        total += part_in[dx].astype(F32)
    aggregated = total.astype(BF)
    pre = jnp.dot(aggregated, weight[...], preferred_element_type=F32)
    square = pre * pre
    bend = jnp.tanh(GELU * (pre + 0.044715 * (square * pre)))
    slope = 0.5 * (1.0 + bend) + (0.5 * GELU) * pre * (1.0 - bend * bend) * (1.0 + 3.0 * 0.044715 * square)
    grad_pre = (cotangent[...].astype(F32) * slope).astype(BF)
    gt[0] = lax.dot_general(weight[...], grad_pre, (((1,), (1,)), ((), ())), preferred_element_type=F32).astype(BF)
    for dx in (2, 1, 3):
        sends.start(("gt", dx), gt.at[0], gt.at[NX - dx], device(0, 0, 0, dx))
    activation[...] = (0.5 * pre * (1.0 + bend)).astype(BF)
    term = lax.dot_general(aggregated, grad_pre, (((0,), (0,)), ((), ())), preferred_element_type=F32)
    for q in range(NX):
        for j in range(8):
            w1[q, j] = term[q * 32 + j % 4 * 8:q * 32 + j % 4 * 8 + 8, j // 4 * 128:j // 4 * 128 + 128]
    for dx in (2, 1, 3):
        sends.start(("w1", dx), w1.at[(x + dx) % NX], w1_in.at[dx], device(0, 0, 0, dx))
    for dx in (1, 3, 2):
        sends.wait(("gt", dx))

    def backward(first, second, other):
        def step(number, carry):
            dzi = first + (second - first) * number
            for dyi in range(NY):
                where = column(dzi, dyi, other)
                sum_ = jnp.zeros((F, ROWS), F32)
                for dx in range(NX):
                    base = (x + dx) % NX * 2 * 128 + where
                    corners = [merged[pick(index, 0, base + a, TCAP)] for a in (0, 1, 128, 129)]
                    grid = jnp.concatenate([jnp.concatenate(corners[:2], axis=1), jnp.concatenate(corners[2:], axis=1)], axis=0)
                    sum_ += jnp.dot(gt[dx], grid, preferred_element_type=F32)
                if other:
                    twin[dzi, dyi] = sum_.astype(BF)
                else:
                    summed[dzi, dyi] = (sum_ + twin_in[dzi, dyi].astype(F32)).astype(BF)
            return carry

        lax.fori_loop(0, 1 if first == second else 2, step, 0)

    r1, r1a, r1b = pl.ds(0, R1), pl.ds(0, R1A), pl.ds(R1A, R1 - R1A)
    r2, r2a, r2b = pl.ds(R1, R2), pl.ds(R1, R2A), pl.ds(R1 + R2A, R2 - R2A)
    dys = (1, 3, 2)

    def for_twin(*group):
        backward(group[0], group[-1], 1)
        for dzi in group:
            sends.start(("t", dzi), twin.at[dzi], twin_in.at[dzi], sibling)

    def for_plane(*group):
        for dzi in group:
            sends.wait(("t", dzi))
        backward(group[0], group[-1], 0)
        for dzi in group:
            for k, dy in enumerate(dys):
                sends.start(("Y", dzi, k), summed.at[dzi, dy, r1], y_in.at[dzi, k], device(0, dy))
        for dzi in group:
            for dy in range(NY):
                if dzi == 4:
                    sends.start(("half", 0, dy), summed.at[4, dy, r2a], half_in.at[0, dy, pl.ds(0, R2A)], device(2, 0))
                    sends.start(("half", 1, dy), summed.at[4, dy, r2b], half_in.at[1, dy, pl.ds(0, R2 - R2A)], device(-2, 0))
                elif dzi in (3, 5):
                    s = 0 if dzi == 3 else 1
                    sends.start(("far", s, dy), summed.at[dzi, dy, r2], far_in.at[s, dy], device(1 - 2 * s, 0))
                elif dzi in (1, 7):
                    s = 0 if dzi == 1 else 1
                    sends.start(("q", s, dy), summed.at[dzi, dy, r2], relay_in.at[s, dy], device(1 - 2 * s, 0))

    def relays():
        for s, dzi in ((0, 2), (1, 6)):
            for dy in (1, 3, 2, 0):
                sends.wait(("half", s, dy))
                sends.wait(("far", s, dy))
                relay[s, dy] = (summed[dzi, dy, r2].astype(F32) + far_in[s, dy].astype(F32)).astype(BF)
                some = pl.ds(0, R2A) if s == 0 else pl.ds(R2A, R2 - R2A)
                extra = half_in[s, dy, pl.ds(0, R2A if s == 0 else R2 - R2A)]
                mine = r2a if s == 0 else r2b
                relay[s, dy, some] = (
                    summed[dzi, dy, mine].astype(F32) + far_in[s, dy, some].astype(F32) + extra.astype(F32)
                ).astype(BF)
                sends.start(("q", 2 + s, dy), relay.at[s, dy], relay_in.at[2 + s, dy], device(2 - 4 * s, 0))

    def y_sum(dzi):
        value = summed[dzi, 0, r1].astype(F32)
        for k in range(3):
            sends.wait(("Y", dzi, k))
            value += y_in[dzi, k].astype(F32)
        return value

    def z_stage(dzi):
        value = y_sum(dzi)
        if dzi in (2, 6):
            s = 0 if dzi == 2 else 1
            sends.wait(("Zfar", s))
            sends.wait(("Zhalf", s))
            value += z_far[s].astype(F32)
            some, size = (r1a, R1A) if s == 0 else (r1b, R1 - R1A)
            z_out[dzi] = value.astype(BF)
            extra = z_half[s, pl.ds(0, size)].astype(F32)
            z_out[dzi, some] = (value[some.start:some.start + size] + extra).astype(BF)
        else:
            z_out[dzi] = value.astype(BF)
        if dzi == 4:
            sends.start(("Zhalf", 0), z_out.at[4, r1a], z_half.at[0, pl.ds(0, R1A)], device(2, 0))
            sends.start(("Zhalf", 1), z_out.at[4, r1b], z_half.at[1, pl.ds(0, R1 - R1A)], device(-2, 0))
        elif dzi in (3, 5):
            s = 0 if dzi == 3 else 1
            sends.start(("Zfar", s), z_out.at[dzi], z_far.at[s], device(1 - 2 * s, 0))
        else:
            sends.start(("Z", dzi), z_out.at[dzi], z_in.at[dzi], device(dzi, 0))

    def q_sum(dy):
        value = summed[0, dy, r2].astype(F32)
        for k in range(4):
            sends.wait(("q", k, dy))
            value += relay_in[k, dy].astype(F32)
        return value

    for_twin(4)
    w2[...] = w1[x]
    for dx in (1, 3, 2):
        sends.wait(("w1", dx))
        w2[...] += w1_in[dx]
    for step in range(1, 8):
        sends.start(("w2", step), w2.at[(mine8 + step) % 8], w2_in.at[step], octet(step))
    for_twin(3, 5)
    for_plane(4)
    for_twin(2, 6)
    for_plane(3, 5)
    for_twin(1, 7)
    for_plane(2, 6)
    here = w2[mine8]
    for step in range(1, 8):
        sends.wait(("w2", step))
        here += w2_in[step]
    w3[z] = here
    for dz in range(1, NZ):
        sends.start(("w3", dz), w3.at[z], w3.at[z], device(dz, 0))
    relays()
    z_stage(4)
    for_twin(0)
    for_plane(1, 7)
    for_plane(0)
    z_stage(3)
    z_stage(5)
    for dz in range(1, NZ):
        sends.wait_for(("w3", dz), w3.at[(z + NZ - dz) % NZ])
    here = w3[0]
    for k in range(1, NZ):
        here += w3[k]
    w4[mine8] = here
    for step in range(1, 8):
        sends.start(("w4", step), w4.at[mine8], w4.at[mine8], octet(step))
    z_stage(2)
    z_stage(6)
    for k, dy in enumerate(dys):
        q_out[k] = q_sum(dy).astype(BF)
        sends.start(("Q", k), q_out.at[k], q_in.at[k], device(0, dy))
    for step in range(1, 8):
        sends.wait_for(("w4", step), w4.at[(mine8 + 8 - step) % 8])
    w5[x] = w4[...]
    for dx in (2, 1, 3):
        sends.start(("w5", dx), w4, w5.at[x], device(0, 0, 0, dx))
    z_stage(1)
    z_stage(7)
    top = y_sum(0)
    bottom = q_sum(0)
    for dzi in (2, 6, 1, 7):
        sends.wait(("Z", dzi))
        top += z_in[dzi].astype(F32)
    for k in range(3):
        sends.wait(("Q", k))
        bottom += q_in[k].astype(F32)
    grad_turned[0:R1] = top
    grad_turned[R1:F] = bottom
    for dx in (1, 3, 2):
        sends.wait_for(("w5", dx), w5.at[(x + NX - dx) % NX])
    sends.drain()
    assert not sends.landing


def finish(active, turned, pieces, activation, grad_features, grad_weight):
    activation[...] = active[...]
    grad_features[...] = turned[...].T
    for q in range(NX):
        for j in range(8):
            grad_weight[q * 32 + j % 4 * 8:q * 32 + j % 4 * 8 + 8, j // 4 * 128:j // 4 * 128 + 128] = pieces[q, j]


def body(features, weight, tiles, tile_rows, tile_cols, tile_count, block_perm, cotangent):
    vmem = pl.BlockSpec(memory_space=pltpu.VMEM)
    parts = pl.pallas_call(
        whole,
        out_shape=(
            jax.ShapeDtypeStruct((ROWS, H), BF),
            jax.ShapeDtypeStruct((F, ROWS), F32),
            jax.ShapeDtypeStruct((NX, 8, 8, 128), F32),
        ),
        in_specs=[pl.BlockSpec(memory_space=pltpu.HBM)] * 8,
        out_specs=(vmem, vmem, vmem),
        scratch_shapes=[
            pltpu.VMEM((F, H), BF),
            pltpu.VMEM((1, TCAP), jnp.int32),
            pltpu.VMEM((1, TCAP), jnp.int32),
            pltpu.VMEM((1, 1), jnp.int32),
            pltpu.VMEM((1, NBLK), jnp.int32),
            pltpu.VMEM((ROWS, H), BF),
            pltpu.VMEM((TCAP, BS, BS), BF),
            pltpu.VMEM((TCAP + 1, BS, BS), BF),
            pltpu.VMEM((8, NPLACE), jnp.int32),
            pltpu.SMEM((8, NPLACE), jnp.int32),
            pltpu.VMEM((NZ, NY, 2, ROWS, F), BF),
            pltpu.VMEM((ROWBLK, BS, F), F32),
            pltpu.VMEM((NX, ROWS, F), BF),
            pltpu.VMEM((NX, ROWS, F), BF),
            pltpu.VMEM((NX, F, ROWS), BF),
            pltpu.VMEM((NZ, NY, F, ROWS), BF),
            pltpu.VMEM((NZ, NY, F, ROWS), BF),
            pltpu.VMEM((NZ, NY, F, ROWS), BF),
            pltpu.VMEM((NZ, 3, R1, ROWS), BF),
            pltpu.VMEM((NZ, R1, ROWS), BF),
            pltpu.VMEM((NZ, R1, ROWS), BF),
            pltpu.VMEM((2, R1, ROWS), BF),
            pltpu.VMEM((2, R1 - R1A, ROWS), BF),
            pltpu.VMEM((2, NY, R2, ROWS), BF),
            pltpu.VMEM((2, NY, R2 - R2A, ROWS), BF),
            pltpu.VMEM((2, NY, R2, ROWS), BF),
            pltpu.VMEM((4, NY, R2, ROWS), BF),
            pltpu.VMEM((3, R2, ROWS), BF),
            pltpu.VMEM((3, R2, ROWS), BF),
            pltpu.VMEM((NX, 8, 8, 128), F32),
            pltpu.VMEM((NX, 8, 8, 128), F32),
            pltpu.VMEM((8, 8, 128), F32),
            pltpu.VMEM((8, 8, 128), F32),
            pltpu.VMEM((NZ, 8, 128), F32),
            pltpu.VMEM((8, 8, 128), F32),
            pltpu.SemaphoreType.DMA((16,)),
            pltpu.SemaphoreType.DMA((NSEM,)),
            pltpu.SemaphoreType.DMA((NSEM,)),
        ],
        compiler_params=pltpu.CompilerParams(
            collective_id=0, has_side_effects=True, vmem_limit_bytes=56 * 2**20),
    )(
        features, weight, tiles, tile_rows.reshape(1, TCAP), tile_cols.reshape(1, TCAP), tile_count,
        block_perm.reshape(1, NBLK), cotangent,
    )
    return pl.pallas_call(
        finish,
        out_shape=(
            jax.ShapeDtypeStruct((ROWS, H), BF),
            jax.ShapeDtypeStruct((ROWS, F), F32),
            jax.ShapeDtypeStruct((F, H), F32),
        ),
    )(*parts)


def solution(mesh):
    return jax.shard_map(
        body,
        mesh=mesh,
        in_specs=(
            P(("row", "col"), None),
            P(),
            P("row", "col", None, None, None),
            P("row", "col", None),
            P("row", "col", None),
            P("row", "col"),
            P(),
            P(("row", "col"), None),
        ),
        out_specs=(P(("row", "col"), None), P(("row", "col"), None), P()),
        check_vma=False,
    )
```

```python
import math

import jax
import jax.numpy as jnp
from jax import lax
from jax.experimental import pallas as pl
from jax.experimental.pallas import tpu as pltpu
from jax.sharding import PartitionSpec as P

MESH = pl.DeviceIdType.MESH
BF = jnp.bfloat16
F32 = jnp.float32

NZ, NY, NX = 8, 4, 4
BS, F, H = 128, 128, 256
TCAP, NBLK, ROWBLK = 384, 512, 8
NPLACE = 1024
ROWS = 256
G1, G1A, G2A, G2 = 144, 64, 48, 112
R1, R1A, R2A, R2 = 80, 32, 16, 48
NSEM = 256
GELU = math.sqrt(2.0 / math.pi)


class Sends:
    def __init__(self, send_sem, recv_sem, device):
        self.send_sem, self.recv_sem, self.device = send_sem, recv_sem, device
        self.count, self.started, self.landing = 0, [], {}

    def describe(self, number, source, target, device):
        return pltpu.make_async_remote_copy(
            src_ref=source, dst_ref=target, send_sem=self.send_sem.at[number],
            recv_sem=self.recv_sem.at[number], device_id=device, device_id_type=MESH)

    def start(self, name, source, target, device):
        copy = self.describe(self.count, source, target, device)
        copy.start()
        self.started.append(copy)
        self.landing[name] = (self.count, target)
        self.count += 1

    def wait(self, name):
        self.wait_for(name, self.landing[name][1])

    def wait_for(self, name, target):
        number, _ = self.landing.pop(name)
        self.describe(number, target, target, self.device).wait_recv()

    def drain(self):
        for copy in self.started:
            copy.wait_send()
        self.started = []


def prepare(rows_ref, cols_ref, count_ref, perm_ref, table):
    def iota(shape, dim):
        return lax.broadcasted_iota(jnp.int32, shape, dim)

    def total(picked, values, axis):
        return jnp.sum(jnp.where(picked, values, 0), axis=axis, keepdims=True)

    square = (TCAP, TCAP)
    sub, lane = iota(square, 0), iota(square, 1)
    cols = total(sub == lane, cols_ref[...], 1)
    rows = total(sub == lane, rows_ref[...], 1)
    spot = total(perm_ref[...] == cols, iota((TCAP, NBLK), 1), 1)
    key = rows * 128 + spot // 8 * 2 + spot % 2
    key = jnp.where(iota((TCAP, 1), 0) < count_ref[...], key, 2048)
    flat = total(sub == lane, key, 0)
    ahead = (flat < key) | ((flat == key) & (lane < sub))
    rank = total(ahead, 1, 1)
    order = total(rank == lane, sub, 0)
    keys = total(rank == lane, key, 0)
    place = iota((TCAP, NPLACE), 1)
    upto = total(key <= place, 1, 0)
    here = total(key == place, 1, 0)
    last = jnp.where(here > 0, upto - 1, TCAP)
    table[...] = jnp.zeros_like(table)
    table[0:1, :] = jnp.clip(last, 0, TCAP)
    table[1:2, 0:TCAP] = jnp.clip(order, 0, TCAP - 1)
    table[2:3, 0:TCAP] = keys


def pick(index, line, number, most):
    return jnp.minimum(jnp.maximum(index[line, number], 0), most)


def merge(index, raw, merged):
    def step(number, carry):
        total, before = carry
        mine = index[2, number]
        keep = jnp.where(mine == before, 1.0, 0.0).astype(F32)
        total = raw[pick(index, 1, number, TCAP - 1)].astype(F32) + total * keep
        merged[number] = total.astype(BF)
        return total, mine

    lax.fori_loop(0, TCAP, step, (jnp.zeros((BS, BS), F32), jnp.int32(-1)), unroll=8)
    merged[TCAP] = jnp.zeros((BS, BS), BF)


def whole(
    features, weight_in, tiles, rows_in, cols_in, count_in, perm_in, cotangent_in,
    activation, grad_turned, w5,
    weight, rows_ref, cols_ref, count_ref, perm_ref, cotangent, raw, merged, table, index, near, acc, part, part_in, gt, twin, twin_in, summed,
    y_in, z_out, z_in, z_far, z_half, far_in, half_in, relay, relay_in, q_out, q_in,
    w1, w1_in, w2, w2_in, w3, w4, local_sem, send_sem, recv_sem,
):
    row, x = lax.axis_index("row"), lax.axis_index("col")
    z, y, core = row // (2 * NY), (row // 2) % NY, row % 2

    def device(dz, dy, dc=0, dx=0):
        there = ((z + dz + NZ) % NZ * NY + (y + dy + NY) % NY) * 2 + (core + dc) % 2
        return there, (x + dx) % NX

    mine8 = y * 2 + core

    def octet(step):
        there = (mine8 + step) % 8
        return (z * NY + there // 2) * 2 + there % 2, x

    lists = [(rows_in, rows_ref), (cols_in, cols_ref), (count_in, count_ref), (perm_in, perm_ref)]
    lists = [pltpu.make_async_copy(*pair, local_sem.at[9 + k]) for k, pair in enumerate(lists)]
    for copy in lists:
        copy.start()
    barrier = pltpu.get_barrier_semaphore()
    peers = [device(dz, 0) for dz in range(1, NZ)] + [octet(step) for step in range(1, 8)]
    peers += [device(0, 0, 0, dx) for dx in range(1, NX)]
    for peer in peers:
        pl.semaphore_signal(barrier, inc=1, device_id=peer, device_id_type=MESH)
    fetches = [pltpu.make_async_copy(features, near.at[0, 0, 0], local_sem.at[13])]
    for part_no in range(8):
        some = pl.ds(part_no * (TCAP // 8), TCAP // 8)
        fetches.append(pltpu.make_async_copy(tiles.at[0, 0, some], raw.at[some], local_sem.at[part_no]))
    fetches.append(pltpu.make_async_copy(weight_in, weight, local_sem.at[14]))
    fetches.append(pltpu.make_async_copy(cotangent_in, cotangent, local_sem.at[15]))
    for fetch in fetches:
        fetch.start()
    for copy in lists:
        copy.wait()
    prepare(rows_ref, cols_ref, count_ref, perm_ref, table)
    to_scalar = pltpu.make_async_copy(table, index, local_sem.at[8])
    to_scalar.start()
    acc[...] = jnp.zeros_like(acc)
    pl.semaphore_wait(barrier, len(peers))

    sends = Sends(send_sem, recv_sem, device(0, 0, 1))
    sibling = device(0, 0, 1)

    def block(oz, oy, piece):
        return near.at[oz % NZ, oy % NY, 0, pl.ds(piece[0], piece[1]), :]

    g1, g1a, g1b = (0, G1), (0, G1A), (G1A, G1 - G1A)
    g2, g2a, g2b = (G1, G2), (G1, G2A), (G1 + G2A, G2 - G2A)

    def pass_on(name, oz, oy, piece, dz, dy):
        source = features.at[pl.ds(piece[0], piece[1]), :] if (oz, oy) == (0, 0) else block(oz, oy, piece)
        sends.start(name, source, block(oz - dz, oy - dy, piece), device(dz, dy))

    def along_y(oz, relayed):
        for dy in (1, -1):
            pass_on(("y", oz, dy), oz, 0, g1, 0, dy)
        if not relayed:
            pass_on(("y", oz, 2), oz, 0, g1, 0, 2)

    def along_y_more(oz):
        for s, half in ((1, g1a), (-1, g1b)):
            sends.wait(("y", oz, s))
            pass_on(("y", oz, 2 * s), oz, -s, half, 0, s)

    def along_y_done(oz, relayed):
        for dy in (2, -2) if relayed else (1, -1, 2):
            sends.wait(("y", oz, dy))

    def along_z(name, oy, piece, dzs):
        for dz in dzs:
            pass_on((name, oy, dz), 0, oy, piece, dz, 0)

    def along_z_more(name, oy, piece, halves):
        for s, half in ((1, halves[0]), (-1, halves[1])):
            sends.wait((name, oy, 2 * s))
            pass_on((name, oy, 3 * s), -2 * s, oy, piece, s, 0)
            pass_on((name, oy, 4 * s), -2 * s, oy, half, 2 * s, 0)

    def q_more(oy):
        along_z_more("q", oy, g2, (g2a, g2b))

    def q_done(*dzs):
        for oy in (0, -1, 1, 2):
            for dz in dzs:
                sends.wait(("q", oy, dz))

    def share(oz):
        sends.start(("s", oz), near.at[oz % NZ, :, 0], near.at[oz % NZ, :, 1], sibling)

    def shared(*ozs):
        for oz in ozs:
            sends.wait(("s", oz))

    def column(dzi, dyi, other):
        there = (((z + dzi) % NZ) * NY + (y + dyi) % NY) * 2 + (core + other) % 2
        return there * 2

    def forward(first, second, other):
        for dzi in (first, second)[:1 if first == second else 2]:
            for part_no in range(0, ROWBLK, 4):
                sum_ = jnp.zeros((4 * BS, F), F32)
                for dyi in range(NY):
                    where = column(dzi, dyi, other)
                    left = [merged[pick(index, 0, rb * 128 + where, TCAP)] for rb in range(part_no, part_no + 4)]
                    right = [merged[pick(index, 0, rb * 128 + where + 1, TCAP)] for rb in range(part_no, part_no + 4)]
                    both = jnp.concatenate([jnp.concatenate(left, axis=0), jnp.concatenate(right, axis=0)], axis=1)
                    sum_ += jnp.dot(both, near[dzi, dyi, other], preferred_element_type=F32)
                acc[pl.ds(part_no, 4)] += sum_.reshape(4, BS, F)

    along_z("z", 0, g1, (2, -2, 1, -1))
    for s in (1, -1):
        pass_on(("p", s), 0, 0, g2, 0, s)
    along_y(0, True)
    pass_on(("p", 2), 0, 0, g2, 0, 2)
    along_z("q", 0, g2, (2, -2, 1, -1))
    to_scalar.wait()
    for fetch in fetches:
        fetch.wait()
    merge(index, raw, merged)
    for s in (1, -1):
        sends.wait(("z", 0, s))
        along_y(-s, True)
    along_z_more("z", 0, g1, (g1a, g1b))
    for s in (1, -1):
        sends.wait(("p", s))
        along_z("q", -s, g2, (2, -2, 1, -1))
    sends.wait(("p", 2))
    along_z("q", 2, g2, (2, -2, 1, -1))
    for s in (1, -1):
        along_y(2 * s, True)
    along_y_more(0)
    q_more(0)
    along_y_more(-1)
    along_y_more(1)
    for s in (1, -1):
        sends.wait(("z", 0, 3 * s))
        along_y(-3 * s, False)
    for s in (1, -1):
        sends.wait(("z", 0, 4 * s))
    along_y(4, False)
    q_more(-1)
    q_more(1)
    along_y_done(0, True)
    share(0)
    along_y_more(-2)
    along_y_more(2)
    q_more(2)
    forward(0, 0, 0)
    q_done(1, -1)
    for oz in (-1, 1):
        along_y_done(oz, True)
        share(oz)
    shared(0)
    forward(0, 0, 1)
    forward(1, 7, 0)
    for oz in (-2, 2):
        along_y_done(oz, True)
        share(oz)
    shared(1, -1)
    forward(1, 7, 1)
    forward(2, 6, 0)
    shared(2, -2)
    forward(2, 6, 1)
    q_done(3, -3)
    for oz in (-3, 3):
        along_y_done(oz, False)
        share(oz)
    forward(3, 5, 0)
    q_done(4, -4)
    along_y_done(4, False)
    share(4)
    shared(3, -3)
    forward(3, 5, 1)
    forward(4, 4, 0)
    shared(4)
    forward(4, 4, 1)

    for dx in (2, 1, 3):
        there = (x + dx) % NX
        part[dx] = acc[pl.ds(there * 2, 2)].reshape(ROWS, F).astype(BF)
        sends.start(("part", dx), part.at[dx], part_in.at[dx], device(0, 0, 0, dx))
    total = acc[pl.ds(x * 2, 2)].reshape(ROWS, F)
    for dx in (1, 3, 2):
        sends.wait(("part", dx))
        total += part_in[dx].astype(F32)
    aggregated = total.astype(BF)
    pre = jnp.dot(aggregated, weight[...], preferred_element_type=F32)
    square = pre * pre
    bend = jnp.tanh(GELU * (pre + 0.044715 * (square * pre)))
    slope = 0.5 * (1.0 + bend) + (0.5 * GELU) * pre * (1.0 - bend * bend) * (1.0 + 3.0 * 0.044715 * square)
    grad_pre = (cotangent[...].astype(F32) * slope).astype(BF)
    gt[0] = lax.dot_general(weight[...], grad_pre, (((1,), (1,)), ((), ())), preferred_element_type=F32).astype(BF)
    for dx in (2, 1, 3):
        sends.start(("gt", dx), gt.at[0], gt.at[NX - dx], device(0, 0, 0, dx))
    activation[...] = (0.5 * pre * (1.0 + bend)).astype(BF)
    term = lax.dot_general(aggregated, grad_pre, (((0,), (0,)), ((), ())), preferred_element_type=F32)
    for q in range(NX):
        for j in range(8):
            w1[q, j] = term[q * 32 + j % 4 * 8:q * 32 + j % 4 * 8 + 8, j // 4 * 128:j // 4 * 128 + 128]
    for dx in (2, 1, 3):
        sends.start(("w1", dx), w1.at[(x + dx) % NX], w1_in.at[dx], device(0, 0, 0, dx))
    sends.drain()
    for dx in (1, 3, 2):
        sends.wait(("gt", dx))

    def backward(first, second, other):
        def step(number, carry):
            dzi = first + (second - first) * number
            for dyi in range(NY):
                where = column(dzi, dyi, other)
                sum_ = jnp.zeros((F, ROWS), F32)
                for dx in range(NX):
                    base = (x + dx) % NX * 2 * 128 + where
                    corners = [merged[pick(index, 0, base + a, TCAP)] for a in (0, 1, 128, 129)]
                    grid = jnp.concatenate([jnp.concatenate(corners[:2], axis=1), jnp.concatenate(corners[2:], axis=1)], axis=0)
                    sum_ += jnp.dot(gt[dx], grid, preferred_element_type=F32)
                if other:
                    twin[dzi, dyi] = sum_.astype(BF)
                else:
                    summed[dzi, dyi] = (sum_ + twin_in[dzi, dyi].astype(F32)).astype(BF)
            return carry

        lax.fori_loop(0, 1 if first == second else 2, step, 0)

    r1, r1a, r1b = pl.ds(0, R1), pl.ds(0, R1A), pl.ds(R1A, R1 - R1A)
    r2, r2a, r2b = pl.ds(R1, R2), pl.ds(R1, R2A), pl.ds(R1 + R2A, R2 - R2A)
    dys = (1, 3, 2)

    def for_twin(*group):
        backward(group[0], group[-1], 1)
        for dzi in group:
            sends.start(("t", dzi), twin.at[dzi], twin_in.at[dzi], sibling)

    def for_plane(*group):
        for dzi in group:
            sends.wait(("t", dzi))
        backward(group[0], group[-1], 0)
        for dzi in group:
            for k, dy in enumerate(dys):
                sends.start(("Y", dzi, k), summed.at[dzi, dy, r1], y_in.at[dzi, k], device(0, dy))
        for dzi in group:
            if dzi == 4:
                sends.start(("half", 0), summed.at[4, :, r2a], half_in.at[0, :, pl.ds(0, R2A)], device(2, 0))
                sends.start(("half", 1), summed.at[4, :, r2b], half_in.at[1, :, pl.ds(0, R2 - R2A)], device(-2, 0))
            elif dzi in (3, 5):
                s = 0 if dzi == 3 else 1
                sends.start(("far", s), summed.at[dzi, :, r2], far_in.at[s], device(1 - 2 * s, 0))
            elif dzi in (1, 7):
                s = 0 if dzi == 1 else 1
                sends.start(("q", s), summed.at[dzi, :, r2], relay_in.at[s], device(1 - 2 * s, 0))

    def relays():
        for s, dzi in ((0, 2), (1, 6)):
            sends.wait(("half", s))
            sends.wait(("far", s))
            size = R2A if s == 0 else R2 - R2A
            start = 0 if s == 0 else R2A
            value = summed[dzi, :, r2].astype(F32) + far_in[s].astype(F32)
            relay[s] = value.astype(BF)
            extra = half_in[s, :, pl.ds(0, size)].astype(F32)
            relay[s, :, pl.ds(start, size)] = (value[:, start:start + size] + extra).astype(BF)
            sends.start(("q", 2 + s), relay.at[s], relay_in.at[2 + s], device(2 - 4 * s, 0))

    def y_sum(dzi):
        value = summed[dzi, 0, r1].astype(F32)
        for k in range(3):
            sends.wait(("Y", dzi, k))
            value += y_in[dzi, k].astype(F32)
        return value

    def z_stage(dzi):
        value = y_sum(dzi)
        if dzi in (2, 6):
            s = 0 if dzi == 2 else 1
            sends.wait(("Zfar", s))
            sends.wait(("Zhalf", s))
            value += z_far[s].astype(F32)
            some, size = (r1a, R1A) if s == 0 else (r1b, R1 - R1A)
            z_out[dzi] = value.astype(BF)
            extra = z_half[s, pl.ds(0, size)].astype(F32)
            z_out[dzi, some] = (value[some.start:some.start + size] + extra).astype(BF)
        else:
            z_out[dzi] = value.astype(BF)
        if dzi == 4:
            sends.start(("Zhalf", 0), z_out.at[4, r1a], z_half.at[0, pl.ds(0, R1A)], device(2, 0))
            sends.start(("Zhalf", 1), z_out.at[4, r1b], z_half.at[1, pl.ds(0, R1 - R1A)], device(-2, 0))
        elif dzi in (3, 5):
            s = 0 if dzi == 3 else 1
            sends.start(("Zfar", s), z_out.at[dzi], z_far.at[s], device(1 - 2 * s, 0))
        else:
            sends.start(("Z", dzi), z_out.at[dzi], z_in.at[dzi], device(dzi, 0))

    def q_sum(dy):
        value = summed[0, dy, r2].astype(F32)
        for k in range(4):
            value += relay_in[k, dy].astype(F32)
        return value

    for_twin(4)
    w2[...] = w1[x]
    for dx in (1, 3, 2):
        sends.wait(("w1", dx))
        w2[...] += w1_in[dx]
    for step in range(1, 8):
        sends.start(("w2", step), w2.at[(mine8 + step) % 8], w2_in.at[step], octet(step))
    for_twin(3, 5)
    for_plane(4)
    for_twin(2, 6)
    for_plane(3, 5)
    for_twin(1, 7)
    for_plane(2, 6)
    here = w2[mine8]
    for step in range(1, 8):
        sends.wait(("w2", step))
        here += w2_in[step]
    w3[z] = here
    for dz in range(1, NZ):
        sends.start(("w3", dz), w3.at[z], w3.at[z], device(dz, 0))
    relays()
    z_stage(4)
    for_twin(0)
    for_plane(1, 7)
    for_plane(0)
    z_stage(3)
    z_stage(5)
    for dz in range(1, NZ):
        sends.wait_for(("w3", dz), w3.at[(z + NZ - dz) % NZ])
    here = w3[0]
    for k in range(1, NZ):
        here += w3[k]
    w4[mine8] = here
    for step in range(1, 8):
        sends.start(("w4", step), w4.at[mine8], w4.at[mine8], octet(step))
    z_stage(2)
    z_stage(6)
    for k in range(4):
        sends.wait(("q", k))
    for k, dy in enumerate(dys):
        q_out[k] = q_sum(dy).astype(BF)
        sends.start(("Q", k), q_out.at[k], q_in.at[k], device(0, dy))
    for step in range(1, 8):
        sends.wait_for(("w4", step), w4.at[(mine8 + 8 - step) % 8])
    w5[x] = w4[...]
    for dx in (2, 1, 3):
        sends.start(("w5", dx), w4, w5.at[x], device(0, 0, 0, dx))
    z_stage(1)
    z_stage(7)
    top = y_sum(0)
    bottom = q_sum(0)
    sends.drain()
    for dzi in (2, 6, 1, 7):
        sends.wait(("Z", dzi))
        top += z_in[dzi].astype(F32)
    for k in range(3):
        sends.wait(("Q", k))
        bottom += q_in[k].astype(F32)
    grad_turned[0:R1] = top
    grad_turned[R1:F] = bottom
    for dx in (1, 3, 2):
        sends.wait_for(("w5", dx), w5.at[(x + NX - dx) % NX])
    sends.drain()
    assert not sends.landing


def finish(active, turned, pieces, activation, grad_features, grad_weight):
    activation[...] = active[...]
    grad_features[...] = turned[...].T
    for q in range(NX):
        for j in range(8):
            grad_weight[q * 32 + j % 4 * 8:q * 32 + j % 4 * 8 + 8, j // 4 * 128:j // 4 * 128 + 128] = pieces[q, j]


def body(features, weight, tiles, tile_rows, tile_cols, tile_count, block_perm, cotangent):
    vmem = pl.BlockSpec(memory_space=pltpu.VMEM)
    parts = pl.pallas_call(
        whole,
        out_shape=(
            jax.ShapeDtypeStruct((ROWS, H), BF),
            jax.ShapeDtypeStruct((F, ROWS), F32),
            jax.ShapeDtypeStruct((NX, 8, 8, 128), F32),
        ),
        in_specs=[pl.BlockSpec(memory_space=pltpu.HBM)] * 8,
        out_specs=(vmem, vmem, vmem),
        scratch_shapes=[
            pltpu.VMEM((F, H), BF),
            pltpu.VMEM((1, TCAP), jnp.int32),
            pltpu.VMEM((1, TCAP), jnp.int32),
            pltpu.VMEM((1, 1), jnp.int32),
            pltpu.VMEM((1, NBLK), jnp.int32),
            pltpu.VMEM((ROWS, H), BF),
            pltpu.VMEM((TCAP, BS, BS), BF),
            pltpu.VMEM((TCAP + 1, BS, BS), BF),
            pltpu.VMEM((8, NPLACE), jnp.int32),
            pltpu.SMEM((8, NPLACE), jnp.int32),
            pltpu.VMEM((NZ, NY, 2, ROWS, F), BF),
            pltpu.VMEM((ROWBLK, BS, F), F32),
            pltpu.VMEM((NX, ROWS, F), BF),
            pltpu.VMEM((NX, ROWS, F), BF),
            pltpu.VMEM((NX, F, ROWS), BF),
            pltpu.VMEM((NZ, NY, F, ROWS), BF),
            pltpu.VMEM((NZ, NY, F, ROWS), BF),
            pltpu.VMEM((NZ, NY, F, ROWS), BF),
            pltpu.VMEM((NZ, 3, R1, ROWS), BF),
            pltpu.VMEM((NZ, R1, ROWS), BF),
            pltpu.VMEM((NZ, R1, ROWS), BF),
            pltpu.VMEM((2, R1, ROWS), BF),
            pltpu.VMEM((2, R1 - R1A, ROWS), BF),
            pltpu.VMEM((2, NY, R2, ROWS), BF),
            pltpu.VMEM((2, NY, R2 - R2A, ROWS), BF),
            pltpu.VMEM((2, NY, R2, ROWS), BF),
            pltpu.VMEM((4, NY, R2, ROWS), BF),
            pltpu.VMEM((3, R2, ROWS), BF),
            pltpu.VMEM((3, R2, ROWS), BF),
            pltpu.VMEM((NX, 8, 8, 128), F32),
            pltpu.VMEM((NX, 8, 8, 128), F32),
            pltpu.VMEM((8, 8, 128), F32),
            pltpu.VMEM((8, 8, 128), F32),
            pltpu.VMEM((NZ, 8, 128), F32),
            pltpu.VMEM((8, 8, 128), F32),
            pltpu.SemaphoreType.DMA((16,)),
            pltpu.SemaphoreType.DMA((NSEM,)),
            pltpu.SemaphoreType.DMA((NSEM,)),
        ],
        compiler_params=pltpu.CompilerParams(
            collective_id=0, has_side_effects=True, vmem_limit_bytes=56 * 2**20),
    )(
        features, weight, tiles, tile_rows.reshape(1, TCAP), tile_cols.reshape(1, TCAP), tile_count,
        block_perm.reshape(1, NBLK), cotangent,
    )
    return pl.pallas_call(
        finish,
        out_shape=(
            jax.ShapeDtypeStruct((ROWS, H), BF),
            jax.ShapeDtypeStruct((ROWS, F), F32),
            jax.ShapeDtypeStruct((F, H), F32),
        ),
    )(*parts)


def solution(mesh):
    return jax.shard_map(
        body,
        mesh=mesh,
        in_specs=(
            P(("row", "col"), None),
            P(),
            P("row", "col", None, None, None),
            P("row", "col", None),
            P("row", "col", None),
            P("row", "col"),
            P(),
            P(("row", "col"), None),
        ),
        out_specs=(P(("row", "col"), None), P(("row", "col"), None), P()),
        check_vma=False,
    )
```
